256 devices in a mesh: dp: 4 (over y_hi, core), expert: 64 (over z, x, y_lo).
Axes of the slice: x: 4, y: 4 (y_hi: 2, y_lo: 2; y = y_hi * 2 + y_lo), z: 8, core: 2. Of those that a mesh axis runs over, the one named last changes fastest.
Arguments:
- patches: bfloat16 [256, 256, 1024], P(('dp', 'expert')), may hold values from -400 to 400
- router: bfloat16 [1024, 128], replicated, may hold values from -1 to 1
- w_in: bfloat16 [128, 1024, 2560], P('expert', None, 'dp'), may hold values from -0.1875 to 0.1875
- w_out: bfloat16 [128, 2560, 1024], P('expert', 'dp'), may hold values from -0.125 to 0.125
- cotangent: bfloat16 [256, 256, 1024], P(('dp', 'expert')), may hold values from -6 to 6
Outputs:
- mixed: bfloat16 [256, 256, 1024], P(('dp', 'expert'))
- grad_patches: bfloat16 [256, 256, 1024], P(('dp', 'expert'))
- grad_router: bfloat16 [1024, 128], P(('dp', 'expert'))
- grad_w_in: bfloat16 [128, 1024, 2560], P('expert', None, 'dp')
- grad_w_out: bfloat16 [128, 2560, 1024], P('expert', 'dp')
The draws below stay inside these ranges and needn't reach their ends.
All inputs are finite; a program needn't handle non-finite values.
Results may differ from the reference program's by a relative error of at most 0.013.
Values may be sent and summed in bfloat16 or wider, within the bound.
A program may use at most 64 MiB of HBM per device.

```python
import math
import jax
import jax.numpy as jnp
from jax import lax

D = 1024
FF = 2560
PATCHES = 256
IMG_DEV = 1
EXPERTS = 128
IMAGES = 256


def draw_patches(key, part):
    key = jax.random.fold_in(key, 11)
    key_noise, key_scale, key_target = jax.random.split(key, 3)
    scales = jnp.exp(jax.random.uniform(key_scale, (IMAGES, PATCHES, 1), minval=math.log(0.4), maxval=math.log(4.0)))
    owners = IMAGES // IMG_DEV
    block_width = D // owners
    owner_ids = jnp.arange(IMAGES) // IMG_DEV
    target = (owner_ids + jax.random.randint(key_target, (), 1, owners + 1)) % owners
    column_ids = jnp.arange(D) // block_width
    emphasis = jnp.where(column_ids[None, :] == target[:, None], 3.0, 1.0)
    noise = jnp.clip(jax.random.normal(key_noise, (IMAGES, PATCHES, D)), -4.0, 4.0)
    values = noise * scales * emphasis[:, None, :]
    return values.astype(jnp.bfloat16)


def draw_router(key, part):
    key = jax.random.fold_in(key, 23)
    key_noise, key_scale = jax.random.split(key, 2)
    noise = jnp.clip(jax.random.normal(key_noise, (D, EXPERTS)), -4.0, 4.0) * D ** (-0.5)
    values = noise * jnp.exp(jax.random.uniform(key_scale, (1, EXPERTS), minval=math.log(0.5), maxval=math.log(2.0)))
    return values.astype(jnp.bfloat16)


def levels(own_key, dims, cuts, smallest, high):
    loudness = 1.0
    for dim, shards_of in cuts:
        steps = jax.random.uniform(jax.random.fold_in(jax.random.fold_in(own_key, 6), dim), (shards_of,), jnp.float32, smallest / len(cuts), high / len(cuts))
        loudness = loudness * jnp.repeat(jnp.exp(steps), dims[dim] // shards_of).reshape((-1,) + (1,) * (len(dims) - 1 - dim))
    return loudness


def gaussian(key, dims, deviation, most, pieces=(), kind=jnp.bfloat16):
    drawn = deviation * jax.random.normal(key, dims, jnp.float32)
    if pieces:
        drawn = drawn * levels(key, dims, pieces, -0.22, 0.18)
    return jnp.clip(drawn, -most, most).astype(kind)


def setup_inputs(seed: int = 0) -> dict:
    keys = jax.random.split(jax.random.key(seed), 6)
    patches = draw_patches(jax.random.fold_in(keys[5], 71), 0)
    router = draw_router(jax.random.fold_in(keys[5], 71), 0)
    w_in = gaussian(keys[2], (EXPERTS, D, FF), D ** -0.5, 0.1875, ((0, 64), (2, 4)))
    w_out = gaussian(keys[3], (EXPERTS, FF, D), FF ** -0.5, 0.125, ((0, 64), (1, 4)))
    cotangent = gaussian(keys[4], (IMAGES, PATCHES, D), 1.0, 6.0, ((0, 256),))
    return {"patches": patches, "router": router, "w_in": w_in, "w_out": w_out, "cotangent": cotangent}


GELU_COEF = math.sqrt(2.0 / math.pi)

def gelu_value(inner):
    return 0.5 * inner * (1.0 + jnp.tanh(GELU_COEF * (inner + 0.044715 * inner * inner * inner)))

def gelu_slope(inner):
    tangent = jnp.tanh(GELU_COEF * (inner + 0.044715 * inner * inner * inner))
    return 0.5 * (1.0 + tangent) + 0.5 * inner * (1.0 - tangent * tangent) * GELU_COEF * (1.0 + 3.0 * 0.044715 * inner * inner)

def expert_forward(operands):
    slots, first_proj, second_proj = operands
    preact = jnp.dot(slots, first_proj, preferred_element_type=jnp.float32)
    hidden = gelu_value(preact).astype(jnp.bfloat16)
    return jnp.dot(hidden, second_proj, preferred_element_type=jnp.float32).astype(jnp.bfloat16)

def expert_backward(operands):
    slots, grad_out, first_proj, second_proj = operands
    preact = jnp.dot(slots, first_proj, preferred_element_type=jnp.float32)
    hidden = gelu_value(preact).astype(jnp.bfloat16)
    grad_hidden = jnp.dot(grad_out, second_proj.T, preferred_element_type=jnp.float32)
    grad_preact = (grad_hidden * gelu_slope(preact)).astype(jnp.bfloat16)
    grad_second = jnp.dot(hidden.T, grad_out, preferred_element_type=jnp.float32).astype(jnp.bfloat16)
    grad_first = jnp.dot(slots.T, grad_preact, preferred_element_type=jnp.float32).astype(jnp.bfloat16)
    grad_slots = jnp.dot(grad_preact, first_proj.T, preferred_element_type=jnp.float32).astype(jnp.bfloat16)
    return (grad_first, grad_second, grad_slots)

def reference(patches, router, w_in, w_out, cotangent):
    patches_wide = patches.astype(jnp.float32)
    router_wide = router.astype(jnp.float32)
    cot_wide = cotangent.astype(jnp.float32)
    logits = jnp.einsum('bmd,de->bme', patches_wide, router_wide)
    dispatch_prob = jax.nn.softmax(logits, axis=1)
    combine_prob = jax.nn.softmax(logits, axis=2)
    dispatch = dispatch_prob.astype(jnp.bfloat16)
    combine = combine_prob.astype(jnp.bfloat16)
    slot_in = jnp.einsum('bme,bmd->bed', dispatch.astype(jnp.float32), patches_wide).astype(jnp.bfloat16)
    slots_major = jnp.swapaxes(slot_in, 0, 1)
    slot_out = jnp.swapaxes(lax.map(expert_forward, (slots_major, w_in, w_out)), 0, 1)
    mixed = jnp.einsum('bme,bed->bmd', combine.astype(jnp.float32), slot_out.astype(jnp.float32)).astype(jnp.bfloat16)
    grad_slot_out = jnp.einsum('bme,bmd->bed', combine.astype(jnp.float32), cot_wide).astype(jnp.bfloat16)
    grad_combine = jnp.einsum('bmd,bed->bme', cot_wide, slot_out.astype(jnp.float32))
    grad_logit_c = combine_prob * (grad_combine - lax.optimization_barrier(jnp.sum(combine_prob * grad_combine, axis=2, keepdims=True)))
    grad_w_in, grad_w_out, grad_slots = lax.map(expert_backward, (slots_major, jnp.swapaxes(grad_slot_out, 0, 1), w_in, w_out))
    grad_slot_in = jnp.swapaxes(grad_slots, 0, 1).astype(jnp.float32)
    grad_dispatch = jnp.einsum('bmd,bed->bme', patches_wide, grad_slot_in)
    grad_logit_d = dispatch_prob * (grad_dispatch - lax.optimization_barrier(jnp.sum(dispatch_prob * grad_dispatch, axis=1, keepdims=True)))
    grad_logits = (grad_logit_c + grad_logit_d).astype(jnp.bfloat16)
    grad_patches = jnp.einsum('bme,bed->bmd', dispatch.astype(jnp.float32), grad_slot_in)
    grad_patches = grad_patches + jnp.einsum('bme,de->bmd', grad_logits.astype(jnp.float32), router_wide)
    grad_router = jnp.einsum('bmd,bme->de', patches_wide, grad_logits.astype(jnp.float32)).astype(jnp.bfloat16)
    return (mixed, grad_patches.astype(jnp.bfloat16), grad_router, grad_w_in, grad_w_out)
```

```python
import math

import jax
import jax.numpy as jnp
from jax import lax
from jax.experimental import pallas as pl
from jax.experimental.pallas import tpu as pltpu
from jax.sharding import PartitionSpec as P

MESH = pl.DeviceIdType.MESH
GELU_COEF = math.sqrt(2.0 / math.pi)
F32 = jnp.float32
BF16 = jnp.bfloat16
D, FF, M, E = 1024, 640, 256, 128
NC = 4
W = D // NC


def dot(a, b):
    return jnp.dot(a, b, preferred_element_type=F32)


def dot_t(a, b):
    return lax.dot_general(a, b, (((1,), (1,)), ((), ())), preferred_element_type=F32)


def dot_tl(a, b):
    return lax.dot_general(a, b, (((0,), (0,)), ((), ())), preferred_element_type=F32)


def one_hot(rows, columns, old_of_new):
    new = lax.broadcasted_iota(jnp.int32, (rows, columns), 0)
    old = lax.broadcasted_iota(jnp.int32, (rows, columns), 1)
    return jnp.where(old_of_new(new) == old, 1.0, 0.0).astype(BF16)


def kernel(
    patches_hbm, router_hbm, w_in_hbm, w_out_hbm, cot_hbm,
    mixed_hbm, gp_hbm, gr_ref, gwi_hbm, gwo_hbm,
    patches, router, w_in, w_out, cot, mixed, gp, gwi, gwo,
    perm, pt, router_t, prob_d, prob_c, disp_t, disp, comb,
    s_buf, x1, x2, x3, x4, xf, pre, slope, hid, gpre,
    po, cs, cr, ys, yr, zs, zr, ws, wr, grad_c, grad_d,
    rt, rcs, rcr, rys, ryr, rzs, rzr, rxr,
    in_sem, out_sem, fs_sem, fr_sem, bs_sem, br_sem, rs_sem, rr_sem,
):
    dp = lax.axis_index("dp")
    ex = lax.axis_index("expert")
    yh, c = dp // 2, dp % 2
    z, x, yl = ex // 8, (ex // 2) % 4, ex % 2
    y = yh * 2 + yl

    def at(x=x, y=y, z=z, c=c):
        return {"dp": (y // 2) * 2 + c, "expert": (z * 4 + x) * 2 + y % 2}

    x_ids = [(x + k) % 4 for k in range(1, 4)]
    y_ids = [(y + k) % 4 for k in range(1, 4)]
    z_ids = [(z + k) % 8 for k in range(1, 8)]

    barrier = pltpu.get_barrier_semaphore()
    everyone = (
        [at(x=v) for v in x_ids] + [at(y=v) for v in y_ids]
        + [at(z=v) for v in z_ids] + [at(c=1 - c)]
    )
    for other in everyone:
        pl.semaphore_signal(barrier, inc=1, device_id=other, device_id_type=MESH)

    loads = [
        pltpu.make_async_copy(src, dst, in_sem.at[i])
        for i, (src, dst) in enumerate(
            [(patches_hbm, patches), (router_hbm, router), (cot_hbm, cot), (w_in_hbm, w_in), (w_out_hbm, w_out)]
        )
    ]
    for load in loads:
        load.start()

    def send(src, dst, ssem, rsem, other):
        pltpu.make_async_remote_copy(
            src_ref=src, dst_ref=dst, send_sem=ssem, recv_sem=rsem, device_id=other, device_id_type=MESH
        ).start()

    def wait(ref, sem):
        pltpu.make_async_copy(ref, ref, sem).wait()

    def rows(start, size):
        return pl.ds(pl.multiple_of(start, size), size)

    def cols(k):
        return slice(k * W, (k + 1) * W)

    perm[0] = one_hot(E, E, lambda i: (i % 4) * 32 + (i // 16) * 4 + (i // 4) % 4)
    perm[1] = one_hot(E, E, lambda i: ((i // 4) % 8) * 16 + (i // 32) * 4 + i % 4)
    perm[2] = one_hot(E, E, lambda i: ((i // 4) % 8) * 16 + (i % 4) * 4 + i // 32)
    perm[3] = one_hot(E, E, lambda i: ((i // 4) % 4) * 32 + (i // 16) * 4 + i % 4)
    perm[4] = one_hot(E, E, lambda i: ((i // 4) % 8) * 16 + (i // 32) * 4 + i % 4)

    loads[1].wait()
    router_t[...] = dot_t(perm[4], router[...]).astype(BF16)
    loads[0].wait()
    logits = dot_t(router_t[...], patches[...])
    e_d = jnp.exp(logits - jnp.max(logits, axis=1, keepdims=True))
    p_d = e_d / jnp.sum(e_d, axis=1, keepdims=True)
    prob_d[...] = p_d
    disp_t[0] = p_d.astype(BF16)

    def f0(p, k):
        rhs = patches if p == 0 else cot
        s_buf[p, k] = dot(disp_t[p], rhs[:, cols(k)]).astype(BF16)

    def f1(p, k):
        for v in x_ids:
            send(s_buf.at[p, k, rows(v * 32, 32)], x1.at[p, k, rows(x * 32, 32)], fs_sem.at[p, k, 0], fr_sem.at[p, k, 0], at(x=v))
        x1[p, k, rows(x * 32, 32), :] = s_buf[p, k, rows(x * 32, 32), :]

    def f2(p, k):
        wait(x1.at[p, k, pl.ds(0, 96)], fr_sem.at[p, k, 0])
        x2[p, k] = dot(perm[0], x1[p, k]).astype(BF16)
        for v in z_ids:
            send(x2.at[p, k, rows(v * 16, 16)], x3.at[p, k, rows(z * 16, 16)], fs_sem.at[p, k, 1], fr_sem.at[p, k, 1], at(z=v))
        x3[p, k, rows(z * 16, 16), :] = x2[p, k, rows(z * 16, 16), :]

    def f3(p, k):
        wait(x3.at[p, k, pl.ds(0, 112)], fr_sem.at[p, k, 1])
        x4[p, k] = dot(perm[1], x3[p, k]).astype(BF16).reshape(4, 32, W)
        mine = rows(c * 128 + y * 32, 32)
        for v in y_ids:
            send(x4.at[p, k, pl.ds((v % 2) * 2, 2)], xf.at[p, k, :, mine], fs_sem.at[p, k, 2], fr_sem.at[p, k, 2], at(y=v))
        for s in range(2):
            xf[p, k, s, mine, :] = x4[p, k, yl * 2 + s]

    def f4(p, k):
        wait(xf.at[p, k, :, pl.ds(0, 96)], fr_sem.at[p, k, 2])
        half = xf.at[p, k, :, rows(c * 128, 128)]
        send(half, half, fs_sem.at[p, k, 3], fr_sem.at[p, k, 3], at(c=1 - c))

    def f5(p, k):
        wait(xf.at[p, k, :, pl.ds(0, 128)], fr_sem.at[p, k, 3])
        for s in range(2):
            if p == 0:
                term = dot(xf[0, k, s], w_in[s, cols(k), :])
            else:
                term = dot_t(xf[1, k, s], w_out[s, :, cols(k)])
            if k == 0:
                pre[p, s] = term
            else:
                pre[p, s] += term

    def gelu():
        for s in range(2):
            def block(i, carry):
                r = rows(i * 32, 32)
                v = pre[0, s, r, :]
                t = jnp.tanh(GELU_COEF * (v + 0.044715 * v * v * v))
                hid[s, r, :] = (0.5 * v * (1.0 + t)).astype(BF16)
                slope[s, r, :] = 0.5 * (1.0 + t) + 0.5 * v * (1.0 - t * t) * GELU_COEF * (1.0 + 3.0 * 0.044715 * v * v)
                return carry
            lax.fori_loop(0, 8, block, 0)

    def grad_pre():
        for s in range(2):
            def block(i, carry):
                r = rows(i * 32, 32)
                gpre[s, r, :] = (pre[1, s, r, :] * slope[s, r, :]).astype(BF16)
                return carry
            lax.fori_loop(0, 8, block, 0)

    def g1(p, k):
        for s in range(2):
            if p == 0:
                po[p, k, s] = dot(hid[s], w_out[s, :, cols(k)])
            else:
                po[p, k, s] = dot_t(gpre[s], w_in[s, cols(k), :])
            cs[p, k, s] = po[p, k, s, rows((1 - c) * 128, 128), :].astype(BF16)
        send(cs.at[p, k], cr.at[p, k], bs_sem.at[p, k, 0], br_sem.at[p, k, 0], at(c=1 - c))

    def g2(p, k):
        wait(cr.at[p, k], br_sem.at[p, k, 0])
        for s in range(2):
            total = (po[p, k, s, rows(c * 128, 128), :] + cr[p, k, s].astype(F32)).astype(BF16)
            for v in range(4):
                ys[p, k, v, s] = total[v * 32:(v + 1) * 32]
        for v in y_ids:
            send(ys.at[p, k, v], yr.at[p, k, y], bs_sem.at[p, k, 1], br_sem.at[p, k, 1], at(y=v))
        yr[p, k, y] = ys[p, k, y]

    def g3(p, k):
        wait(yr.at[p, k, pl.ds(0, 3)], br_sem.at[p, k, 1])
        total = (yr[p, k, 0:2].astype(F32) + yr[p, k, 2:4].astype(F32)).astype(BF16).reshape(E, W)
        zs[p, k] = dot(perm[3], total).astype(BF16)
        for v in z_ids:
            send(zs.at[p, k, rows(v * 16, 16)], zr.at[p, k, rows(z * 16, 16)], bs_sem.at[p, k, 2], br_sem.at[p, k, 2], at(z=v))
        zr[p, k, rows(z * 16, 16), :] = zs[p, k, rows(z * 16, 16), :]

    def g4(p, k):
        wait(zr.at[p, k, pl.ds(0, 112)], br_sem.at[p, k, 2])
        ws[p, k] = dot(perm[2], zr[p, k]).astype(BF16)
        for v in x_ids:
            send(ws.at[p, k, rows(v * 32, 32)], wr.at[p, k, rows(x * 32, 32)], bs_sem.at[p, k, 3], br_sem.at[p, k, 3], at(x=v))
        wr[p, k, rows(x * 32, 32), :] = ws[p, k, rows(x * 32, 32), :]

    def g5(p, k):
        wait(wr.at[p, k, pl.ds(0, 96)], br_sem.at[p, k, 3])
        if p == 0:
            mixed[:, cols(k)] = dot(comb[...], wr[0, k]).astype(BF16)
            term = dot_t(wr[0, k], cot[:, cols(k)])
            acc = grad_c
        else:
            term = dot_t(wr[1, k], patches[:, cols(k)])
            acc = grad_d
        if k == 0:
            acc[...] = term
        else:
            acc[...] += term

    def w_out_grad(k):
        for s in range(2):
            gwo[s, :, cols(k)] = dot_tl(hid[s], xf[1, k, s]).astype(BF16)

    def w_in_grad(k):
        for s in range(2):
            gwi[s, cols(k), :] = dot_tl(xf[0, k, s], gpre[s]).astype(BF16)

    def combine_probs():
        e_c = jnp.exp(logits - jnp.max(logits, axis=0, keepdims=True))
        p_c = e_c / jnp.sum(e_c, axis=0, keepdims=True)
        prob_c[...] = p_c
        disp_t[1] = p_c.astype(BF16)

    def images_side():
        disp[...] = disp_t[0].T
        comb[...] = disp_t[1].T
        pick = one_hot(M, M, lambda i: ((i // 16) % 8) * 32 + ((i // 4) % 4) * 8 + (i // 128) * 4 + i % 4)
        for cc in range(2):
            for hh in range(2):
                pt[cc * 512 + hh * 256:cc * 512 + (hh + 1) * 256] = dot_t(
                    pick, patches[:, hh * 512 + cc * 256:hh * 512 + (cc + 1) * 256]
                ).astype(BF16)

    outs = {}

    def put(name, src, dst, i):
        outs[name] = pltpu.make_async_copy(src, dst, out_sem.at[i])
        outs[name].start()

    for k in range(NC):
        f0(0, k)
        if k == 0:
            pl.semaphore_wait(barrier, len(everyone))
        f1(0, k)
    combine_probs()
    loads[2].wait()
    f0(1, 0)
    f0(1, 1)
    f0(1, 2)
    f0(1, 3)
    f2(0, 0)
    f2(0, 1)
    f2(0, 2)
    f2(0, 3)
    f3(0, 0)
    f1(1, 0)
    f3(0, 1)
    f1(1, 1)
    f4(0, 0)
    f3(0, 2)
    f1(1, 2)
    f4(0, 1)
    f3(0, 3)
    f1(1, 3)
    images_side()
    f2(1, 0)
    f4(0, 2)
    f2(1, 1)
    loads[3].wait()
    f5(0, 0)
    f4(0, 3)
    f2(1, 2)
    f5(0, 1)
    f3(1, 0)
    f5(0, 2)
    f2(1, 3)
    f5(0, 3)
    gelu()
    loads[4].wait()
    g1(0, 0)
    f3(1, 1)
    f4(1, 0)
    g1(0, 1)
    g2(0, 0)
    f3(1, 2)
    f4(1, 1)
    g1(0, 2)
    g2(0, 1)
    f3(1, 3)
    f4(1, 2)
    f5(1, 0)
    g1(0, 3)
    g2(0, 2)
    f4(1, 3)
    g3(0, 0)
    f5(1, 1)
    g2(0, 3)
    g3(0, 1)
    f5(1, 2)
    f5(1, 3)
    grad_pre()
    g1(1, 0)
    g3(0, 2)
    g1(1, 1)
    g2(1, 0)
    g3(0, 3)
    g1(1, 2)
    g2(1, 1)
    g4(0, 0)
    g1(1, 3)
    g2(1, 2)
    g4(0, 1)
    g3(1, 0)
    g2(1, 3)
    g4(0, 2)
    w_out_grad(0)
    w_out_grad(1)
    g3(1, 1)
    g4(0, 3)
    w_out_grad(2)
    w_out_grad(3)
    g3(1, 2)
    put("gwo", gwo, gwo_hbm, 0)
    g5(0, 0)
    g5(0, 1)
    g3(1, 3)
    g5(0, 2)
    g5(0, 3)
    put("mixed", mixed, mixed_hbm, 1)
    g4(1, 0)
    w_in_grad(0)
    g4(1, 1)
    w_in_grad(1)
    g4(1, 2)
    w_in_grad(2)
    w_in_grad(3)
    put("gwi", gwi, gwi_hbm, 2)
    p_c = prob_c[...]
    g_c = grad_c[...]
    grad_c[...] = p_c * (g_c - jnp.sum(p_c * g_c, axis=0, keepdims=True))
    g4(1, 3)
    g5(1, 0)
    g5(1, 1)
    g5(1, 2)
    g5(1, 3)
    p_d = prob_d[...]
    g_d = grad_d[...]
    g_t = (grad_c[...] + p_d * (g_d - jnp.sum(p_d * g_d, axis=1, keepdims=True))).astype(BF16)

    rt[...] = dot_t(pt[...], g_t)
    rcs[...] = rt[rows((1 - c) * 512, 512), :].astype(BF16)
    send(rcs, rcr, rs_sem.at[0], rr_sem.at[0], at(c=1 - c))
    g_m = g_t.T
    for k in range(2):
        gp[:, cols(k)] = (dot(disp[...], wr[1, k]) + dot(g_m, router_t[:, cols(k)])).astype(BF16)
    wait(rcr, rr_sem.at[0])
    rys[...] = (rt[rows(c * 512, 512), :] + rcr[...].astype(F32)).astype(BF16).reshape(4, 128, 128)
    for v in y_ids:
        send(rys.at[v], ryr.at[y], rs_sem.at[1], rr_sem.at[1], at(y=v))
    ryr[y] = rys[y]
    for k in range(2, 4):
        gp[:, cols(k)] = (dot(disp[...], wr[1, k]) + dot(g_m, router_t[:, cols(k)])).astype(BF16)
    put("gp", gp, gp_hbm, 3)
    wait(ryr.at[pl.ds(0, 3)], rr_sem.at[1])
    rzs[...] = jnp.sum(ryr[...].astype(F32), axis=0).reshape(8, 16, 128)
    for v in z_ids:
        send(rzs.at[v], rzr.at[z], rs_sem.at[2], rr_sem.at[2], at(z=v))
    rzr[z] = rzs[z]
    wait(rzr.at[pl.ds(0, 7)], rr_sem.at[2])
    rxr[x] = jnp.sum(rzr[...], axis=0)
    for v in x_ids:
        send(rxr.at[x], rxr.at[x], rs_sem.at[3], rr_sem.at[3], at(x=v))
    wait(rxr.at[pl.ds(0, 3)], rr_sem.at[3])
    total = jnp.sum(rxr[...], axis=0).astype(BF16)
    total = dot(total, perm[4])
    mine = jnp.zeros((4, E), F32)
    for v in range(4):
        mine = jnp.where(x == v, total[v * 4:(v + 1) * 4], mine)
    gr_ref[...] = mine.astype(BF16)

    for p in range(2):
        for k in range(NC):
            wait(x1.at[p, k, pl.ds(0, 96)], fs_sem.at[p, k, 0])
            wait(x3.at[p, k, pl.ds(0, 112)], fs_sem.at[p, k, 1])
            wait(xf.at[p, k, :, pl.ds(0, 96)], fs_sem.at[p, k, 2])
            wait(xf.at[p, k, :, pl.ds(0, 128)], fs_sem.at[p, k, 3])
            wait(cr.at[p, k], bs_sem.at[p, k, 0])
            wait(yr.at[p, k, pl.ds(0, 3)], bs_sem.at[p, k, 1])
            wait(zr.at[p, k, pl.ds(0, 112)], bs_sem.at[p, k, 2])
            wait(wr.at[p, k, pl.ds(0, 96)], bs_sem.at[p, k, 3])
    wait(rcr, rs_sem.at[0])
    wait(ryr.at[pl.ds(0, 3)], rs_sem.at[1])
    wait(rzr.at[pl.ds(0, 7)], rs_sem.at[2])
    wait(rxr.at[pl.ds(0, 3)], rs_sem.at[3])
    for name in outs:
        outs[name].wait()


def on_device(patches, router, w_in, w_out, cotangent):
    v = pltpu.VMEM
    any_spec = pl.BlockSpec(memory_space=pl.ANY)
    shape = jax.ShapeDtypeStruct
    mixed, gp, gr, gwi, gwo = pl.pallas_call(
        kernel,
        name="soft_moe",
        out_shape=(
            shape((M, D), BF16), shape((M, D), BF16), shape((4, E), BF16), shape((2, D, FF), BF16), shape((2, FF, D), BF16),
        ),
        in_specs=[any_spec] * 5,
        out_specs=(any_spec, any_spec, pl.BlockSpec(memory_space=pltpu.VMEM), any_spec, any_spec),
        scratch_shapes=[
            v((M, D), BF16), v((D, E), BF16), v((2, D, FF), BF16), v((2, FF, D), BF16), v((M, D), BF16),
            v((M, D), BF16), v((M, D), BF16), v((2, D, FF), BF16), v((2, FF, D), BF16),
            v((5, E, E), BF16), v((D, M), BF16), v((E, D), BF16), v((E, M), F32), v((E, M), F32),
            v((2, E, M), BF16), v((M, E), BF16), v((M, E), BF16),
            v((2, NC, E, W), BF16), v((2, NC, E, W), BF16), v((2, NC, E, W), BF16), v((2, NC, E, W), BF16),
            v((2, NC, 4, 32, W), BF16), v((2, NC, 2, 256, W), BF16),
            v((2, 2, 256, FF), F32), v((2, 256, FF), F32), v((2, 256, FF), BF16), v((2, 256, FF), BF16),
            v((2, NC, 2, 256, W), F32), v((2, NC, 2, 128, W), BF16), v((2, NC, 2, 128, W), BF16),
            v((2, NC, 4, 2, 32, W), BF16), v((2, NC, 4, 2, 32, W), BF16),
            v((2, NC, E, W), BF16), v((2, NC, E, W), BF16), v((2, NC, E, W), BF16), v((2, NC, E, W), BF16),
            v((E, M), F32), v((E, M), F32),
            v((D, E), F32), v((512, E), BF16), v((512, E), BF16), v((4, 128, E), BF16), v((4, 128, E), BF16),
            v((8, 16, E), F32), v((8, 16, E), F32), v((4, 16, E), F32),
            pltpu.SemaphoreType.DMA((5,)), pltpu.SemaphoreType.DMA((4,)),
            pltpu.SemaphoreType.DMA((2, NC, 4)), pltpu.SemaphoreType.DMA((2, NC, 4)),
            pltpu.SemaphoreType.DMA((2, NC, 4)), pltpu.SemaphoreType.DMA((2, NC, 4)),
            pltpu.SemaphoreType.DMA((4,)), pltpu.SemaphoreType.DMA((4,)),
        ],
        compiler_params=pltpu.CompilerParams(
            collective_id=0, has_side_effects=True, vmem_limit_bytes=50 * 2**20
        ),
        cost_estimate=pl.CostEstimate(flops=4_700_000_000, bytes_accessed=13_000_000, transcendentals=500_000),
    )(patches[0], router, w_in, w_out, cotangent[0])
    return mixed[None], gp[None], gr, gwi, gwo


def solution(mesh):
    placed = (
        P(("dp", "expert"), None, None),
        P(),
        P("expert", None, "dp"),
        P("expert", "dp", None),
        P(("dp", "expert"), None, None),
    )
    return jax.shard_map(
        on_device,
        mesh=mesh,
        in_specs=placed,
        out_specs=(
            P(("dp", "expert"), None, None),
            P(("dp", "expert"), None, None),
            P(("dp", "expert"), None),
            P("expert", None, "dp"),
            P("expert", "dp", None),
        ),
        check_vma=False,
    )
```

```python
import math

import jax
import jax.numpy as jnp
from jax import lax
from jax.experimental import pallas as pl
from jax.experimental.pallas import tpu as pltpu
from jax.sharding import PartitionSpec as P

MESH = pl.DeviceIdType.MESH
GELU_COEF = math.sqrt(2.0 / math.pi)
F32 = jnp.float32
BF16 = jnp.bfloat16
D, FF, M, E = 1024, 640, 256, 128
W = 256


def dot(a, b):
    return jnp.dot(a, b, preferred_element_type=F32)


def dot_t(a, b):
    return lax.dot_general(a, b, (((1,), (1,)), ((), ())), preferred_element_type=F32)


def dot_tl(a, b):
    return lax.dot_general(a, b, (((0,), (0,)), ((), ())), preferred_element_type=F32)


def one_hot(rows, columns, old_of_new):
    new = lax.broadcasted_iota(jnp.int32, (rows, columns), 0)
    old = lax.broadcasted_iota(jnp.int32, (rows, columns), 1)
    return jnp.where(old_of_new(new) == old, 1.0, 0.0).astype(BF16)


GROUPS = ((0, 1, 7, 2), (6, 3, 5, 4))


def kernel(
    patches_hbm, router_hbm, w_in_hbm, w_out_hbm, cot_hbm,
    mixed, gp, gr_ref, gwi, gwo,
    patches, router, w_in, w_out, cot,
    perm, pt, router_t, prob_d, prob_c, disp_t, disp, comb,
    sr, ms, xr, x4, xf, pre, slope, hid, gpre,
    po, cs, cr, ys, yr, zs, zr, so, grad_c, grad_d,
    rt, rcs, rcr, rys, ryr, rzs, rzr,
    in_sem, fs_sem, fr_sem, bs_sem, br_sem, rs_sem, rr_sem,
):
    dp = lax.axis_index("dp")
    ex = lax.axis_index("expert")
    yh, c = dp // 2, dp % 2
    z, x, yl = ex // 8, (ex // 2) % 4, ex % 2
    y = yh * 2 + yl

    def at(x=x, y=y, z=z, c=c):
        return {"dp": (y // 2) * 2 + c, "expert": (z * 4 + x) * 2 + y % 2}

    y_ids = [(y + k) % 4 for k in range(1, 4)]
    plane = [
        (g, o, (x + k) % 4, dz)
        for g in range(2) for o, dz in enumerate(GROUPS[g]) for k in range(4) if dz or k
    ]

    barrier = pltpu.get_barrier_semaphore()
    everyone = [at(y=v) for v in y_ids] + [at(c=1 - c)] + [at(x=v, z=(z + dz) % 8) for _, _, v, dz in plane]
    for other in everyone:
        pl.semaphore_signal(barrier, inc=1, device_id=other, device_id_type=MESH)

    loads = [
        pltpu.make_async_copy(src, dst, in_sem.at[i])
        for i, (src, dst) in enumerate(
            [(router_hbm, router), (patches_hbm, patches), (cot_hbm, cot), (w_in_hbm, w_in), (w_out_hbm, w_out)]
        )
    ]
    for load in loads:
        load.start()

    def send(src, dst, ssem, rsem, other):
        pltpu.make_async_remote_copy(
            src_ref=src, dst_ref=dst, send_sem=ssem, recv_sem=rsem, device_id=other, device_id_type=MESH
        ).start()

    def wait(ref, sem):
        pltpu.make_async_copy(ref, ref, sem).wait()

    def rows(start, size):
        return pl.ds(pl.multiple_of(start, size), size)

    def cols(k):
        return slice(k * W, (k + 1) * W)

    perm[0] = one_hot(M, M, lambda i: ((i // 4) % 4) * 64 + (i // 16) * 4 + i % 4)
    perm[1] = one_hot(M, M, lambda i: (i % 16) * 16 + i // 16)
    perm[2] = one_hot(M, M, lambda i: ((i // 4) % 16) * 16 + (i // 64) * 4 + i % 4)
    perm[3] = one_hot(M, M, lambda i: (i % 16) * 16 + i // 16)

    loads[0].wait()
    router_t[...] = dot_t(one_hot(E, E, lambda i: i), router[...]).astype(BF16)
    loads[1].wait()
    logits = dot_t(router_t[...], patches[...])
    e_d = jnp.exp(logits - jnp.max(logits, axis=1, keepdims=True))
    p_d = e_d / jnp.sum(e_d, axis=1, keepdims=True)
    prob_d[...] = p_d
    disp_t[0] = p_d.astype(BF16)

    def f0(p):
        rhs = patches if p == 0 else cot
        for k in range(4):
            part = dot(disp_t[p], rhs[:, cols(k)]).astype(BF16)
            for h in range(2):
                sr[p, h, k * 64:(k + 1) * 64] = part[h * 64:(h + 1) * 64]
        for h in range(2):
            ms[p, h * 16:(h + 1) * 16] = dot(perm[0], sr[p, h]).astype(BF16).reshape(16, 16, W)

    def f1(p):
        for g, o, v, dz in plane:
            to = (z + 8 - dz) % 8
            send(ms.at[p, to * 4 + v], xr.at[p, g, o * 4 + x], fs_sem.at[p, g, 0], fr_sem.at[p, g, 0], at(x=v, z=to))
        xr[p, 0, x] = ms[p, z * 4 + x]

    def f3(p, g):
        wait(xr.at[p, g, pl.ds(0, 15 + g)], fr_sem.at[p, g, 0])
        moved = dot(perm[1], xr[p, g].reshape(M, W)).astype(BF16)
        for k in range(4):
            for q in range(4):
                x4[p, g, q, :, cols(k)] = moved[(k * 4 + q) * 16:(k * 4 + q + 1) * 16]
        mine = rows(g * 128 + c * 64 + y * 16, 16)
        for v in y_ids:
            send(x4.at[p, g, pl.ds((v % 2) * 2, 2)], xf.at[p, :, mine], fs_sem.at[p, g, 1], fr_sem.at[p, g, 1], at(y=v))
        for s in range(2):
            xf[p, s, mine, :] = x4[p, g, yl * 2 + s]

    def f4(p, g):
        wait(xf.at[p, :, pl.ds(0, 48)], fr_sem.at[p, g, 1])
        half = xf.at[p, :, rows(g * 128 + c * 64, 64)]
        send(half, half, fs_sem.at[p, g, 2], fr_sem.at[p, g, 2], at(c=1 - c))

    def f5(p, g):
        wait(xf.at[p, :, pl.ds(0, 64)], fr_sem.at[p, g, 2])
        r = slice(g * 128, (g + 1) * 128)
        for s in range(2):
            if p == 0:
                pre[0, s, r] = dot(xf[0, s, r], w_in[s])
            else:
                pre[1, s, r] = dot_t(xf[1, s, r], w_out[s])

    def gelu(g):
        for s in range(2):
            def block(i, carry):
                r = rows(g * 128 + i * 32, 32)
                v = pre[0, s, r, :]
                t = jnp.tanh(GELU_COEF * (v + 0.044715 * v * v * v))
                hid[s, r, :] = (0.5 * v * (1.0 + t)).astype(BF16)
                slope[s, r, :] = 0.5 * (1.0 + t) + 0.5 * v * (1.0 - t * t) * GELU_COEF * (1.0 + 3.0 * 0.044715 * v * v)
                return carry
            lax.fori_loop(0, 4, block, 0)

    def grad_pre(g):
        for s in range(2):
            def block(i, carry):
                r = rows(g * 128 + i * 32, 32)
                gpre[s, r, :] = (pre[1, s, r, :] * slope[s, r, :]).astype(BF16)
                return carry
            lax.fori_loop(0, 4, block, 0)

    def g1(p, g):
        r = slice(g * 128, (g + 1) * 128)
        for s in range(2):
            if p == 0:
                po[p, g, s] = dot(hid[s, r], w_out[s])
            else:
                po[p, g, s] = dot_t(gpre[s, r], w_in[s])
            cs[p, g, s] = po[p, g, s, rows((1 - c) * 64, 64), :].astype(BF16)
        send(cs.at[p, g], cr.at[p, g], bs_sem.at[p, g, 0], br_sem.at[p, g, 0], at(c=1 - c))

    def g2(p, g):
        wait(cr.at[p, g], br_sem.at[p, g, 0])
        for s in range(2):
            total = (po[p, g, s, rows(c * 64, 64), :] + cr[p, g, s].astype(F32)).astype(BF16)
            for v in range(4):
                ys[p, g, v, s] = total[v * 16:(v + 1) * 16]
        for v in y_ids:
            send(ys.at[p, g, v], yr.at[p, g, y], bs_sem.at[p, g, 1], br_sem.at[p, g, 1], at(y=v))
        yr[p, g, y] = ys[p, g, y]

    def g3(p, g):
        wait(yr.at[p, g, pl.ds(0, 3)], br_sem.at[p, g, 1])
        total = (yr[p, g, 0:2].astype(F32) + yr[p, g, 2:4].astype(F32)).astype(BF16).reshape(64, D)
        stacked = jnp.concatenate([total[:, cols(k)] for k in range(4)], axis=0)
        zs[p, g] = dot(perm[3], stacked).astype(BF16).reshape(16, 16, W)
        for h, o, v, dz in plane:
            if h == g:
                to = (z + dz) % 8
                send(zs.at[p, g, o * 4 + v], zr.at[p, z * 4 + x], bs_sem.at[p, g, 2], br_sem.at[p, 0, 2], at(x=v, z=to))
        if g == 0:
            zr[p, z * 4 + x] = zs[p, 0, x]

    def g4(p):
        wait(zr.at[p, pl.ds(0, 31)], br_sem.at[p, 0, 2])
        for h in range(2):
            moved = dot(perm[2], zr[p, h * 16:(h + 1) * 16].reshape(M, W)).astype(BF16)
            for k in range(4):
                so[p, h * 64:(h + 1) * 64, cols(k)] = moved[k * 64:(k + 1) * 64]

    def w_out_grad(k):
        for s in range(2):
            gwo[s, :, cols(k)] = dot_tl(hid[s], xf[1, s, :, cols(k)]).astype(BF16)

    def w_in_grad(k):
        for s in range(2):
            gwi[s, cols(k), :] = dot_tl(xf[0, s, :, cols(k)], gpre[s]).astype(BF16)

    def combine_probs():
        e_c = jnp.exp(logits - jnp.max(logits, axis=0, keepdims=True))
        p_c = e_c / jnp.sum(e_c, axis=0, keepdims=True)
        prob_c[...] = p_c
        disp_t[1] = p_c.astype(BF16)

    def images_side():
        disp[...] = disp_t[0].T
        comb[...] = disp_t[1].T
        pick = one_hot(M, M, lambda i: ((i // 16) % 8) * 32 + ((i // 4) % 4) * 8 + (i // 128) * 4 + i % 4)
        for cc in range(2):
            for hh in range(2):
                pt[cc * 512 + hh * 256:cc * 512 + (hh + 1) * 256] = dot_t(
                    pick, patches[:, hh * 512 + cc * 256:hh * 512 + (cc + 1) * 256]
                ).astype(BF16)

    f0(0)
    pl.semaphore_wait(barrier, len(everyone))
    f1(0)
    combine_probs()
    loads[2].wait()
    f0(1)
    f1(1)
    images_side()
    f3(0, 0)
    f3(0, 1)
    f4(0, 0)
    loads[3].wait()
    f5(0, 0)
    gelu(0)
    f3(1, 0)
    f4(0, 1)
    loads[4].wait()
    g1(0, 0)
    f5(0, 1)
    gelu(1)
    g1(0, 1)
    f3(1, 1)
    g2(0, 0)
    f4(1, 0)
    g2(0, 1)
    f5(1, 0)
    grad_pre(0)
    g1(1, 0)
    f4(1, 1)
    g3(0, 0)
    g2(1, 0)
    f5(1, 1)
    grad_pre(1)
    g1(1, 1)
    g3(0, 1)
    g2(1, 1)
    w_out_grad(0)
    w_out_grad(1)
    g3(1, 0)
    w_out_grad(2)
    w_out_grad(3)
    g3(1, 1)
    w_in_grad(0)
    w_in_grad(1)
    g4(0)
    mixed[...] = dot(comb[...], so[0]).astype(BF16)
    p_c = prob_c[...]
    g_c = dot_t(so[0], cot[...])
    grad_c[...] = p_c * (g_c - jnp.sum(p_c * g_c, axis=0, keepdims=True))
    w_in_grad(2)
    w_in_grad(3)
    g4(1)
    p_d = prob_d[...]
    g_d = dot_t(so[1], patches[...])
    g_t = (grad_c[...] + p_d * (g_d - jnp.sum(p_d * g_d, axis=1, keepdims=True))).astype(BF16)

    rt[...] = dot_t(pt[...], g_t)
    rcs[...] = rt[rows((1 - c) * 512, 512), :].astype(BF16)
    send(rcs, rcr, rs_sem.at[0], rr_sem.at[0], at(c=1 - c))
    g_m = g_t.T
    for k in range(2):
        gp[:, cols(k)] = (dot(disp[...], so[1, :, cols(k)]) + dot(g_m, router_t[:, cols(k)])).astype(BF16)
    wait(rcr, rr_sem.at[0])
    rys[...] = (rt[rows(c * 512, 512), :] + rcr[...].astype(F32)).astype(BF16).reshape(4, 128, 128)
    for v in y_ids:
        send(rys.at[v], ryr.at[y], rs_sem.at[1], rr_sem.at[1], at(y=v))
    ryr[y] = rys[y]
    for k in range(2, 4):
        gp[:, cols(k)] = (dot(disp[...], so[1, :, cols(k)]) + dot(g_m, router_t[:, cols(k)])).astype(BF16)
    wait(ryr.at[pl.ds(0, 3)], rr_sem.at[1])
    total = jnp.sum(ryr[...].astype(F32), axis=0)
    for b in range(32):
        rzs[b] = total[b * 4:(b + 1) * 4]
    for g, o, v, dz in plane:
        to = (z + dz) % 8
        send(rzs.at[to * 4 + v], rzr.at[z * 4 + x], rs_sem.at[2], rr_sem.at[2], at(x=v, z=to))
    rzr[z * 4 + x] = rzs[z * 4 + x]
    wait(rzr.at[pl.ds(0, 31)], rr_sem.at[2])
    gr_ref[...] = jnp.sum(rzr[...], axis=0).astype(BF16)

    for p in range(2):
        for g in range(2):
            wait(xr.at[p, g, pl.ds(0, 15 + g)], fs_sem.at[p, g, 0])
            wait(xf.at[p, :, pl.ds(0, 48)], fs_sem.at[p, g, 1])
            wait(xf.at[p, :, pl.ds(0, 64)], fs_sem.at[p, g, 2])
            wait(cr.at[p, g], bs_sem.at[p, g, 0])
            wait(yr.at[p, g, pl.ds(0, 3)], bs_sem.at[p, g, 1])
            wait(zs.at[p, g, pl.ds(0, 15 + g)], bs_sem.at[p, g, 2])
    wait(rcr, rs_sem.at[0])
    wait(ryr.at[pl.ds(0, 3)], rs_sem.at[1])
    wait(rzr.at[pl.ds(0, 31)], rs_sem.at[2])


def store(*refs):
    sem = refs[-1]
    copies = [pltpu.make_async_copy(refs[i], refs[5 + i], sem.at[i]) for i in range(5)]
    for copy in copies:
        copy.start()
    for copy in copies:
        copy.wait()


def on_device(patches, router, w_in, w_out, cotangent):
    v = pltpu.VMEM
    any_spec = pl.BlockSpec(memory_space=pl.ANY)
    shapes = ((M, D), (M, D), (4, E), (2, D, FF), (2, FF, D))
    args = [
        pltpu.with_memory_space_constraint(a, pltpu.HBM)
        for a in (patches[0], router, w_in, w_out, cotangent[0])
    ]
    results = pl.pallas_call(
        kernel,
        name="soft_moe",
        out_shape=tuple(v(s, BF16) for s in shapes),
        in_specs=[any_spec] * 5,
        out_specs=[pl.BlockSpec(memory_space=pltpu.VMEM)] * 5,
        scratch_shapes=[
            v((M, D), BF16), v((D, E), BF16), v((2, D, FF), BF16), v((2, FF, D), BF16), v((M, D), BF16),
            v((4, M, M), BF16), v((D, M), BF16), v((E, D), BF16), v((E, M), F32), v((E, M), F32),
            v((2, E, M), BF16), v((M, E), BF16), v((M, E), BF16),
            v((2, 2, M, W), BF16), v((2, 32, 16, W), BF16), v((2, 2, 16, 16, W), BF16), v((2, 2, 4, 16, D), BF16),
            v((2, 2, 256, D), BF16),
            v((2, 2, 256, FF), F32), v((2, 256, FF), F32), v((2, 256, FF), BF16), v((2, 256, FF), BF16),
            v((2, 2, 2, 128, D), F32), v((2, 2, 2, 64, D), BF16), v((2, 2, 2, 64, D), BF16),
            v((2, 2, 4, 2, 16, D), BF16), v((2, 2, 4, 2, 16, D), BF16),
            v((2, 2, 16, 16, W), BF16), v((2, 32, 16, W), BF16), v((2, E, D), BF16),
            v((E, M), F32), v((E, M), F32),
            v((D, E), F32), v((512, E), BF16), v((512, E), BF16), v((4, 128, E), BF16), v((4, 128, E), BF16),
            v((32, 4, E), F32), v((32, 4, E), F32),
            pltpu.SemaphoreType.DMA((5,)),
            pltpu.SemaphoreType.DMA((2, 2, 3)), pltpu.SemaphoreType.DMA((2, 2, 3)),
            pltpu.SemaphoreType.DMA((2, 2, 3)), pltpu.SemaphoreType.DMA((2, 2, 3)),
            pltpu.SemaphoreType.DMA((3,)), pltpu.SemaphoreType.DMA((3,)),
        ],
        compiler_params=pltpu.CompilerParams(
            collective_id=0, has_side_effects=True, vmem_limit_bytes=44 * 2**20
        ),
        cost_estimate=pl.CostEstimate(flops=4_700_000_000, bytes_accessed=13_000_000, transcendentals=500_000),
    )(*args)
    mixed, gp, gr, gwi, gwo = pl.pallas_call(
        store,
        name="store",
        out_shape=tuple(jax.ShapeDtypeStruct(s, BF16) for s in shapes),
        in_specs=[pl.BlockSpec(memory_space=pltpu.VMEM)] * 5,
        out_specs=[any_spec] * 5,
        scratch_shapes=[pltpu.SemaphoreType.DMA((5,))],
        compiler_params=pltpu.CompilerParams(vmem_limit_bytes=4 * 2**20),
    )(*[pltpu.with_memory_space_constraint(a, pltpu.VMEM) for a in results])
    return mixed[None], gp[None], gr, gwi, gwo


def solution(mesh):
    placed = (
        P(("dp", "expert"), None, None),
        P(),
        P("expert", None, "dp"),
        P("expert", "dp", None),
        P(("dp", "expert"), None, None),
    )
    return jax.shard_map(
        on_device,
        mesh=mesh,
        in_specs=placed,
        out_specs=(
            P(("dp", "expert"), None, None),
            P(("dp", "expert"), None, None),
            P(("dp", "expert"), None),
            P("expert", None, "dp"),
            P("expert", "dp", None),
        ),
        check_vma=False,
    )
```

```python
import math

import jax
import jax.numpy as jnp
from jax import lax
from jax.experimental import pallas as pl
from jax.experimental.pallas import tpu as pltpu
from jax.sharding import PartitionSpec as P

MESH = pl.DeviceIdType.MESH
GELU_COEF = math.sqrt(2.0 / math.pi)
F32 = jnp.float32
BF16 = jnp.bfloat16
D, FF, M, E = 1024, 640, 256, 128
W = 256


def dot(a, b):
    return jnp.dot(a, b, preferred_element_type=F32)


def dot_t(a, b):
    return lax.dot_general(a, b, (((1,), (1,)), ((), ())), preferred_element_type=F32)


def dot_tl(a, b):
    return lax.dot_general(a, b, (((0,), (0,)), ((), ())), preferred_element_type=F32)


def one_hot(rows, columns, old_of_new):
    new = lax.broadcasted_iota(jnp.int32, (rows, columns), 0)
    old = lax.broadcasted_iota(jnp.int32, (rows, columns), 1)
    return jnp.where(old_of_new(new) == old, 1.0, 0.0).astype(BF16)


GROUPS = ((0, 1, 7, 2), (6, 3, 5, 4))


def kernel(
    patches_hbm, router_hbm, w_in_hbm, w_out_hbm, cot_hbm,
    mixed, gp, gr_ref, gwi, gwo,
    patches, router, w_in, w_out, cot,
    perm, pt, prob_d, prob_c, disp_t, disp, comb,
    sr, ms, xr, x4, xf, pre, slope, hid, gpre,
    po, cs, cr, ys, yr, zs, zr, so, grad_c,
    rt, rcs, rcr, rys, ryr, rzs, rzr,
    in_sem, fs_sem, fr_sem, bs_sem, br_sem, rs_sem, rr_sem,
):
    dp = lax.axis_index("dp")
    ex = lax.axis_index("expert")
    yh, c = dp // 2, dp % 2
    z, x, yl = ex // 8, (ex // 2) % 4, ex % 2
    y = yh * 2 + yl

    def at(x=x, y=y, z=z, c=c):
        return {"dp": (y // 2) * 2 + c, "expert": (z * 4 + x) * 2 + y % 2}

    y_ids = [(y + k) % 4 for k in range(1, 4)]
    plane = [
        (g, o, (x + k) % 4, dz)
        for g in range(2) for o, dz in enumerate(GROUPS[g]) for k in range(4) if dz or k
    ]

    barrier = pltpu.get_barrier_semaphore()
    everyone = [at(y=v) for v in y_ids] + [at(c=1 - c)] + [at(x=v, z=(z + dz) % 8) for _, _, v, dz in plane]
    for other in everyone:
        pl.semaphore_signal(barrier, inc=1, device_id=other, device_id_type=MESH)

    loads = [
        pltpu.make_async_copy(src, dst, in_sem.at[i])
        for i, (src, dst) in enumerate(
            [(router_hbm, router), (patches_hbm, patches), (cot_hbm, cot), (w_in_hbm, w_in), (w_out_hbm, w_out)]
        )
    ]
    for load in loads[:3]:
        load.start()

    def send(src, dst, ssem, rsem, other):
        pltpu.make_async_remote_copy(
            src_ref=src, dst_ref=dst, send_sem=ssem, recv_sem=rsem, device_id=other, device_id_type=MESH
        ).start()

    def wait(ref, sem):
        pltpu.make_async_copy(ref, ref, sem).wait()

    def rows(start, size):
        return pl.ds(pl.multiple_of(start, size), size)

    def cols(k):
        return slice(k * W, (k + 1) * W)

    perm[0] = one_hot(M, M, lambda i: ((i // 4) % 4) * 64 + (i // 16) * 4 + i % 4)
    perm[1] = one_hot(M, M, lambda i: (i % 16) * 16 + i // 16)
    perm[2] = one_hot(M, M, lambda i: ((i // 4) % 16) * 16 + (i // 64) * 4 + i % 4)
    perm[3] = one_hot(M, M, lambda i: (i % 16) * 16 + i // 16)

    loads[0].wait()
    loads[1].wait()
    logits = dot(patches[...], router[...])
    e_d = jnp.exp(logits - jnp.max(logits, axis=0, keepdims=True))
    p_d = e_d / jnp.sum(e_d, axis=0, keepdims=True)
    prob_d[...] = p_d
    disp[...] = p_d.astype(BF16)
    disp_t[0] = disp[...].T

    def f0(p):
        rhs = patches if p == 0 else cot
        for k in range(4):
            part = dot(disp_t[p], rhs[:, cols(k)]).astype(BF16)
            for h in range(2):
                sr[p, h, k * 64:(k + 1) * 64] = part[h * 64:(h + 1) * 64]
        for h in range(2):
            ms[p, h * 16:(h + 1) * 16] = dot(perm[0], sr[p, h]).astype(BF16).reshape(16, 16, W)

    def f1(p):
        for g, o, v, dz in plane:
            to = (z + 8 - dz) % 8
            send(ms.at[p, to * 4 + v], xr.at[p, g, o * 4 + x], fs_sem.at[p, g, 0], fr_sem.at[p, g, 0], at(x=v, z=to))
        xr[p, 0, x] = ms[p, z * 4 + x]

    def f3(p, g):
        wait(xr.at[p, g, pl.ds(0, 15 + g)], fr_sem.at[p, g, 0])
        moved = dot(perm[1], xr[p, g].reshape(M, W)).astype(BF16)
        for k in range(4):
            for q in range(4):
                x4[p, g, q, :, cols(k)] = moved[(k * 4 + q) * 16:(k * 4 + q + 1) * 16]
        mine = rows(g * 128 + c * 64 + y * 16, 16)
        for v in y_ids:
            send(x4.at[p, g, pl.ds((v % 2) * 2, 2)], xf.at[p, :, mine], fs_sem.at[p, g, 1], fr_sem.at[p, g, 1], at(y=v))
        for s in range(2):
            xf[p, s, mine, :] = x4[p, g, yl * 2 + s]

    def f4(p, g):
        wait(xf.at[p, :, pl.ds(0, 48)], fr_sem.at[p, g, 1])
        half = xf.at[p, :, rows(g * 128 + c * 64, 64)]
        send(half, half, fs_sem.at[p, g, 2], fr_sem.at[p, g, 2], at(c=1 - c))

    def f5(p, g):
        wait(xf.at[p, :, pl.ds(0, 64)], fr_sem.at[p, g, 2])
        r = slice(g * 128, (g + 1) * 128)
        for s in range(2):
            if p == 0:
                pre[0, s, r] = dot(xf[0, s, r], w_in[s])
            else:
                pre[1, s, r] = dot_t(xf[1, s, r], w_out[s])

    def gelu(g):
        for s in range(2):
            def block(i, carry):
                r = rows(g * 128 + i * 32, 32)
                v = pre[0, s, r, :]
                t = jnp.tanh(GELU_COEF * (v + 0.044715 * v * v * v))
                hid[s, r, :] = (0.5 * v * (1.0 + t)).astype(BF16)
                slope[s, r, :] = 0.5 * (1.0 + t) + 0.5 * v * (1.0 - t * t) * GELU_COEF * (1.0 + 3.0 * 0.044715 * v * v)
                return carry
            lax.fori_loop(0, 4, block, 0)

    def grad_pre(g):
        for s in range(2):
            def block(i, carry):
                r = rows(g * 128 + i * 32, 32)
                gpre[s, r, :] = (pre[1, s, r, :] * slope[s, r, :]).astype(BF16)
                return carry
            lax.fori_loop(0, 4, block, 0)

    def g1(p, g):
        r = slice(g * 128, (g + 1) * 128)
        for s in range(2):
            if p == 0:
                po[p, g, s] = dot(hid[s, r], w_out[s])
            else:
                po[p, g, s] = dot_t(gpre[s, r], w_in[s])
            cs[p, g, s] = po[p, g, s, rows((1 - c) * 64, 64), :].astype(BF16)
        send(cs.at[p, g], cr.at[p, g], bs_sem.at[p, g, 0], br_sem.at[p, g, 0], at(c=1 - c))

    def g2(p, g):
        wait(cr.at[p, g], br_sem.at[p, g, 0])
        for s in range(2):
            total = (po[p, g, s, rows(c * 64, 64), :] + cr[p, g, s].astype(F32)).astype(BF16)
            for v in range(4):
                ys[p, g, v, s] = total[v * 16:(v + 1) * 16]
        for v in y_ids:
            send(ys.at[p, g, v], yr.at[p, g, y], bs_sem.at[p, g, 1], br_sem.at[p, g, 1], at(y=v))
        yr[p, g, y] = ys[p, g, y]

    def g3(p, g):
        wait(yr.at[p, g, pl.ds(0, 3)], br_sem.at[p, g, 1])
        total = (yr[p, g, 0:2].astype(F32) + yr[p, g, 2:4].astype(F32)).astype(BF16).reshape(64, D)
        stacked = jnp.concatenate([total[:, cols(k)] for k in range(4)], axis=0)
        zs[p, g] = dot(perm[3], stacked).astype(BF16).reshape(16, 16, W)
        for h, o, v, dz in plane:
            if h == g:
                to = (z + dz) % 8
                send(zs.at[p, g, o * 4 + v], zr.at[p, z * 4 + x], bs_sem.at[p, g, 2], br_sem.at[p, 0, 2], at(x=v, z=to))
        if g == 0:
            zr[p, z * 4 + x] = zs[p, 0, x]

    def g4(p):
        wait(zr.at[p, pl.ds(0, 31)], br_sem.at[p, 0, 2])
        for h in range(2):
            moved = dot(perm[2], zr[p, h * 16:(h + 1) * 16].reshape(M, W)).astype(BF16)
            for k in range(4):
                so[p, h * 64:(h + 1) * 64, cols(k)] = moved[k * 64:(k + 1) * 64]

    def w_out_grad(k):
        for s in range(2):
            gwo[s, :, cols(k)] = dot_tl(hid[s], xf[1, s, :, cols(k)]).astype(BF16)

    def w_in_grad(k):
        for s in range(2):
            gwi[s, cols(k), :] = dot_tl(xf[0, s, :, cols(k)], gpre[s]).astype(BF16)

    def combine_probs():
        e_c = jnp.exp(logits - jnp.max(logits, axis=1, keepdims=True))
        p_c = e_c / jnp.sum(e_c, axis=1, keepdims=True)
        prob_c[...] = p_c
        comb[...] = p_c.astype(BF16)
        disp_t[1] = comb[...].T

    def images_side():
        pick = one_hot(M, M, lambda i: ((i // 16) % 8) * 32 + ((i // 4) % 4) * 8 + (i // 128) * 4 + i % 4)
        for cc in range(2):
            for hh in range(2):
                pt[cc * 512 + hh * 256:cc * 512 + (hh + 1) * 256] = dot_t(
                    pick, patches[:, hh * 512 + cc * 256:hh * 512 + (cc + 1) * 256]
                ).astype(BF16)

    f0(0)
    pl.semaphore_wait(barrier, len(everyone))
    f1(0)
    for load in loads[3:]:
        load.start()
    combine_probs()
    loads[2].wait()
    f0(1)
    images_side()
    f3(0, 0)
    f1(1)
    f3(0, 1)
    f4(0, 0)
    f3(1, 0)
    loads[3].wait()
    f5(0, 0)
    gelu(0)
    loads[4].wait()
    g1(0, 0)
    f4(0, 1)
    f3(1, 1)
    g2(0, 0)
    f5(0, 1)
    gelu(1)
    g1(0, 1)
    f4(1, 0)
    g2(0, 1)
    f5(1, 0)
    grad_pre(0)
    f4(1, 1)
    g1(1, 0)
    f5(1, 1)
    grad_pre(1)
    g2(1, 0)
    g1(1, 1)
    g3(0, 0)
    g2(1, 1)
    g3(0, 1)
    w_out_grad(0)
    w_out_grad(1)
    w_out_grad(2)
    w_out_grad(3)
    g3(1, 0)
    w_in_grad(0)
    w_in_grad(1)
    g3(1, 1)
    w_in_grad(2)
    w_in_grad(3)
    g4(0)
    mixed[...] = dot(comb[...], so[0]).astype(BF16)
    p_c = prob_c[...]
    g_c = dot_t(cot[...], so[0])
    grad_c[...] = p_c * (g_c - jnp.sum(p_c * g_c, axis=1, keepdims=True))
    g4(1)
    p_d = prob_d[...]
    g_d = dot_t(patches[...], so[1])
    g_m = (grad_c[...] + p_d * (g_d - jnp.sum(p_d * g_d, axis=0, keepdims=True))).astype(BF16)

    rcs[...] = dot(pt[rows((1 - c) * 512, 512), :], g_m).astype(BF16)
    send(rcs, rcr, rs_sem.at[0], rr_sem.at[0], at(c=1 - c))
    rt[...] = dot(pt[rows(c * 512, 512), :], g_m)
    for k in range(2):
        gp[:, cols(k)] = (dot(disp[...], so[1, :, cols(k)]) + dot_t(g_m, router[cols(k), :])).astype(BF16)
    wait(rcr, rr_sem.at[0])
    rys[...] = (rt[...] + rcr[...].astype(F32)).astype(BF16).reshape(4, 128, 128)
    for v in y_ids:
        send(rys.at[v], ryr.at[y], rs_sem.at[1], rr_sem.at[1], at(y=v))
    ryr[y] = rys[y]
    for k in range(2, 4):
        gp[:, cols(k)] = (dot(disp[...], so[1, :, cols(k)]) + dot_t(g_m, router[cols(k), :])).astype(BF16)
    wait(ryr.at[pl.ds(0, 3)], rr_sem.at[1])
    total = jnp.sum(ryr[...].astype(F32), axis=0)
    for b in range(32):
        rzs[b] = total[b * 4:(b + 1) * 4]
    for g, o, v, dz in plane:
        to = (z + dz) % 8
        send(rzs.at[to * 4 + v], rzr.at[z * 4 + x], rs_sem.at[2], rr_sem.at[2], at(x=v, z=to))
    rzr[z * 4 + x] = rzs[z * 4 + x]
    wait(rzr.at[pl.ds(0, 31)], rr_sem.at[2])
    gr_ref[...] = jnp.sum(rzr[...], axis=0).astype(BF16)

    for p in range(2):
        for g in range(2):
            wait(xr.at[p, g, pl.ds(0, 15 + g)], fs_sem.at[p, g, 0])
            wait(xf.at[p, :, pl.ds(0, 48)], fs_sem.at[p, g, 1])
            wait(xf.at[p, :, pl.ds(0, 64)], fs_sem.at[p, g, 2])
            wait(cr.at[p, g], bs_sem.at[p, g, 0])
            wait(yr.at[p, g, pl.ds(0, 3)], bs_sem.at[p, g, 1])
            wait(zs.at[p, g, pl.ds(0, 15 + g)], bs_sem.at[p, g, 2])
    wait(rcr, rs_sem.at[0])
    wait(ryr.at[pl.ds(0, 3)], rs_sem.at[1])
    wait(rzr.at[pl.ds(0, 31)], rs_sem.at[2])


def store(*refs):
    sem = refs[-1]
    copies = []
    for src, dst in zip(refs[:5], refs[5:10]):
        if src.shape[0] == 2:
            parts = [(src.at[s, pl.ds(h, src.shape[1] // 2)], dst.at[s, pl.ds(h, src.shape[1] // 2)])
                     for s in range(2) for h in (0, src.shape[1] // 2)]
        else:
            parts = [(src, dst)]
        for a, b in parts:
            copies.append(pltpu.make_async_copy(a, b, sem.at[len(copies)]))
            copies[-1].start()
    for copy in copies:
        copy.wait()


def on_device(patches, router, w_in, w_out, cotangent):
    v = pltpu.VMEM
    any_spec = pl.BlockSpec(memory_space=pl.ANY)
    shapes = ((M, D), (M, D), (4, E), (2, D, FF), (2, FF, D))
    args = [
        pltpu.with_memory_space_constraint(a, pltpu.HBM)
        for a in (patches[0], router, w_in, w_out, cotangent[0])
    ]
    results = pl.pallas_call(
        kernel,
        name="soft_moe",
        out_shape=tuple(v(s, BF16) for s in shapes),
        in_specs=[any_spec] * 5,
        out_specs=[pl.BlockSpec(memory_space=pltpu.VMEM)] * 5,
        scratch_shapes=[
            v((M, D), BF16), v((D, E), BF16), v((2, D, FF), BF16), v((2, FF, D), BF16), v((M, D), BF16),
            v((4, M, M), BF16), v((D, M), BF16), v((M, E), F32), v((M, E), F32),
            v((2, E, M), BF16), v((M, E), BF16), v((M, E), BF16),
            v((2, 2, M, W), BF16), v((2, 32, 16, W), BF16), v((2, 2, 16, 16, W), BF16), v((2, 2, 4, 16, D), BF16),
            v((2, 2, 256, D), BF16),
            v((2, 2, 256, FF), F32), v((2, 256, FF), F32), v((2, 256, FF), BF16), v((2, 256, FF), BF16),
            v((2, 2, 2, 128, D), F32), v((2, 2, 2, 64, D), BF16), v((2, 2, 2, 64, D), BF16),
            v((2, 2, 4, 2, 16, D), BF16), v((2, 2, 4, 2, 16, D), BF16),
            v((2, 2, 16, 16, W), BF16), v((2, 32, 16, W), BF16), v((2, E, D), BF16),
            v((M, E), F32),
            v((512, E), F32), v((512, E), BF16), v((512, E), BF16), v((4, 128, E), BF16), v((4, 128, E), BF16),
            v((32, 4, E), F32), v((32, 4, E), F32),
            pltpu.SemaphoreType.DMA((5,)),
            pltpu.SemaphoreType.DMA((2, 2, 3)), pltpu.SemaphoreType.DMA((2, 2, 3)),
            pltpu.SemaphoreType.DMA((2, 2, 3)), pltpu.SemaphoreType.DMA((2, 2, 3)),
            pltpu.SemaphoreType.DMA((3,)), pltpu.SemaphoreType.DMA((3,)),
        ],
        compiler_params=pltpu.CompilerParams(
            collective_id=0, has_side_effects=True, vmem_limit_bytes=44 * 2**20
        ),
        cost_estimate=pl.CostEstimate(flops=4_700_000_000, bytes_accessed=13_000_000, transcendentals=500_000),
    )(*args)
    mixed, gp, gr, gwi, gwo = pl.pallas_call(
        store,
        name="store",
        out_shape=tuple(jax.ShapeDtypeStruct(s, BF16) for s in shapes),
        in_specs=[pl.BlockSpec(memory_space=pltpu.VMEM)] * 5,
        out_specs=[any_spec] * 5,
        scratch_shapes=[pltpu.SemaphoreType.DMA((11,))],
        compiler_params=pltpu.CompilerParams(vmem_limit_bytes=4 * 2**20),
    )(*[pltpu.with_memory_space_constraint(a, pltpu.VMEM) for a in results])
    return mixed[None], gp[None], gr, gwi, gwo


def solution(mesh):
    placed = (
        P(("dp", "expert"), None, None),
        P(),
        P("expert", None, "dp"),
        P("expert", "dp", None),
        P(("dp", "expert"), None, None),
    )
    return jax.shard_map(
        on_device,
        mesh=mesh,
        in_specs=placed,
        out_specs=(
            P(("dp", "expert"), None, None),
            P(("dp", "expert"), None, None),
            P(("dp", "expert"), None),
            P("expert", None, "dp"),
            P("expert", "dp", None),
        ),
        check_vma=False,
    )
```

```python
import math

import jax
import jax.numpy as jnp
from jax import lax
from jax.experimental import pallas as pl
from jax.experimental.pallas import tpu as pltpu
from jax.sharding import PartitionSpec as P

MESH = pl.DeviceIdType.MESH
GELU_COEF = math.sqrt(2.0 / math.pi)
F32 = jnp.float32
BF16 = jnp.bfloat16
D, FF, M, E = 1024, 640, 256, 128
W = 256


def dot(a, b):
    return jnp.dot(a, b, preferred_element_type=F32)


def dot_t(a, b):
    return lax.dot_general(a, b, (((1,), (1,)), ((), ())), preferred_element_type=F32)


def dot_tl(a, b):
    return lax.dot_general(a, b, (((0,), (0,)), ((), ())), preferred_element_type=F32)


def one_hot(rows, columns, old_of_new):
    new = lax.broadcasted_iota(jnp.int32, (rows, columns), 0)
    old = lax.broadcasted_iota(jnp.int32, (rows, columns), 1)
    return jnp.where(old_of_new(new) == old, 1.0, 0.0).astype(BF16)


GROUPS = ((2, 7, 1, 0), (4, 3, 5, 6))
HOME = [(g, o) for g in range(2) for o in range(4) if GROUPS[g][o] == 0][0]


def kernel(
    patches_hbm, router_hbm, w_in_hbm, w_out_hbm, cot_hbm,
    mixed, gp, gr_ref, gwi, gwo,
    patches, router, w_in, w_out, cot,
    perm, pt, prob_d, prob_c, disp_t, disp, comb,
    sr, ms, xr, x4, xf, pre, slope, hid, gpre,
    po, cs, cr, ys, yr, zs, zr, so, grad_c,
    rt, rcs, rcr, rys, ryr, rzs, rzr,
    in_sem, fs_sem, fr_sem, bs_sem, br_sem, rs_sem, rr_sem,
):
    dp = lax.axis_index("dp")
    ex = lax.axis_index("expert")
    yh, c = dp // 2, dp % 2
    z, x, yl = ex // 8, (ex // 2) % 4, ex % 2
    y = yh * 2 + yl

    def at(x=x, y=y, z=z, c=c):
        return {"dp": (y // 2) * 2 + c, "expert": (z * 4 + x) * 2 + y % 2}

    y_ids = [(y + k) % 4 for k in (1, 3, 2)]
    plane = [
        (g, o, (x + k) % 4, dz)
        for g in range(2) for o, dz in enumerate(GROUPS[g]) for k in (2, 1, 3, 0) if dz or k
    ]

    barrier = pltpu.get_barrier_semaphore()
    everyone = [at(y=v) for v in y_ids] + [at(c=1 - c)] + [at(x=v, z=(z + dz) % 8) for _, _, v, dz in plane]
    for other in everyone:
        pl.semaphore_signal(barrier, inc=1, device_id=other, device_id_type=MESH)

    loads = [
        pltpu.make_async_copy(src, dst, in_sem.at[i])
        for i, (src, dst) in enumerate(
            [(router_hbm, router), (patches_hbm, patches), (cot_hbm, cot), (w_in_hbm, w_in), (w_out_hbm, w_out)]
        )
    ]
    for load in loads[:3]:
        load.start()

    def send(src, dst, ssem, rsem, other):
        pltpu.make_async_remote_copy(
            src_ref=src, dst_ref=dst, send_sem=ssem, recv_sem=rsem, device_id=other, device_id_type=MESH
        ).start()

    def wait(ref, sem):
        pltpu.make_async_copy(ref, ref, sem).wait()

    def rows(start, size):
        return pl.ds(pl.multiple_of(start, size), size)

    def cols(k):
        return slice(k * W, (k + 1) * W)

    perm[0] = one_hot(M, M, lambda i: ((i // 4) % 4) * 64 + (i // 16) * 4 + i % 4)
    perm[1] = one_hot(M, M, lambda i: (i % 16) * 16 + i // 16)
    perm[2] = one_hot(M, M, lambda i: ((i // 4) % 16) * 16 + (i // 64) * 4 + i % 4)
    perm[3] = one_hot(M, M, lambda i: (i % 16) * 16 + i // 16)

    loads[0].wait()
    loads[1].wait()
    logits = dot(patches[...], router[...])
    e_d = jnp.exp(logits - jnp.max(logits, axis=0, keepdims=True))
    p_d = e_d / jnp.sum(e_d, axis=0, keepdims=True)
    prob_d[...] = p_d
    disp[...] = p_d.astype(BF16)
    disp_t[0] = disp[...].T

    def f0(p):
        rhs = patches if p == 0 else cot
        for k in range(4):
            part = dot(disp_t[p], rhs[:, cols(k)]).astype(BF16)
            for h in range(2):
                sr[p, h, k * 64:(k + 1) * 64] = part[h * 64:(h + 1) * 64]
        for h in range(2):
            ms[p, h * 16:(h + 1) * 16] = dot(perm[0], sr[p, h]).astype(BF16).reshape(16, 16, W)

    def f1(p):
        for g, o, v, dz in plane:
            to = (z + 8 - dz) % 8
            send(ms.at[p, to * 4 + v], xr.at[p, g, o * 4 + x], fs_sem.at[p, g, 0], fr_sem.at[p, g, 0], at(x=v, z=to))
        xr[p, HOME[0], HOME[1] * 4 + x] = ms[p, z * 4 + x]

    def f3(p, g):
        wait(xr.at[p, g, pl.ds(0, 16 - (g == HOME[0]))], fr_sem.at[p, g, 0])
        moved = dot(perm[1], xr[p, g].reshape(M, W)).astype(BF16)
        for k in range(4):
            for q in range(4):
                x4[p, g, q, :, cols(k)] = moved[(k * 4 + q) * 16:(k * 4 + q + 1) * 16]
        mine = rows(g * 128 + c * 64 + y * 16, 16)
        for s in range(2):
            for v in y_ids:
                send(x4.at[p, g, (v % 2) * 2 + s], xf.at[p, s, mine], fs_sem.at[p, g, 1], fr_sem.at[p, g, 1], at(y=v))
            xf[p, s, mine, :] = x4[p, g, yl * 2 + s]
        send(x4.at[p, g, pl.ds(yl * 2, 2)], xf.at[p, :, mine], fs_sem.at[p, g, 2], fr_sem.at[p, g, 2], at(c=1 - c))

    def f4(p, g):
        wait(xf.at[p, :, pl.ds(0, 48)], fr_sem.at[p, g, 1])
        for v in y_ids:
            part = xf.at[p, :, rows(g * 128 + c * 64 + v * 16, 16)]
            send(part, part, fs_sem.at[p, g, 2], fr_sem.at[p, g, 2], at(c=1 - c))

    def f5(p, g):
        wait(xf.at[p, :, pl.ds(0, 64)], fr_sem.at[p, g, 2])
        r = slice(g * 128, (g + 1) * 128)
        for s in range(2):
            if p == 0:
                pre[0, s, r] = dot(xf[0, s, r], w_in[s])
            else:
                pre[1, s, r] = dot_t(xf[1, s, r], w_out[s])

    def gelu(g):
        for s in range(2):
            def block(i, carry):
                r = rows(g * 128 + i * 32, 32)
                v = pre[0, s, r, :]
                t = jnp.tanh(GELU_COEF * (v + 0.044715 * v * v * v))
                hid[s, r, :] = (0.5 * v * (1.0 + t)).astype(BF16)
                slope[s, r, :] = 0.5 * (1.0 + t) + 0.5 * v * (1.0 - t * t) * GELU_COEF * (1.0 + 3.0 * 0.044715 * v * v)
                return carry
            lax.fori_loop(0, 4, block, 0)

    def grad_pre(g):
        for s in range(2):
            def block(i, carry):
                r = rows(g * 128 + i * 32, 32)
                gpre[s, r, :] = (pre[1, s, r, :] * slope[s, r, :]).astype(BF16)
                return carry
            lax.fori_loop(0, 4, block, 0)

    def g1(p, g):
        r = slice(g * 128, (g + 1) * 128)
        for s in range(2):
            if p == 0:
                po[p, g, s] = dot(hid[s, r], w_out[s])
            else:
                po[p, g, s] = dot_t(gpre[s, r], w_in[s])
            cs[p, g, s] = po[p, g, s, rows((1 - c) * 64, 64), :].astype(BF16)
        send(cs.at[p, g], cr.at[p, g], bs_sem.at[p, g, 0], br_sem.at[p, g, 0], at(c=1 - c))

    def g2(p, g):
        wait(cr.at[p, g], br_sem.at[p, g, 0])
        for s in range(2):
            total = (po[p, g, s, rows(c * 64, 64), :] + cr[p, g, s].astype(F32)).astype(BF16)
            for v in range(4):
                ys[p, g, v, s] = total[v * 16:(v + 1) * 16]
        for s in range(2):
            for v in y_ids:
                send(ys.at[p, g, v, s], yr.at[p, g, y, s], bs_sem.at[p, g, 1], br_sem.at[p, g, 1], at(y=v))
        yr[p, g, y] = ys[p, g, y]

    def g3(p, g):
        wait(yr.at[p, g, pl.ds(0, 3)], br_sem.at[p, g, 1])
        total = (yr[p, g, 0:2].astype(F32) + yr[p, g, 2:4].astype(F32)).astype(BF16).reshape(64, D)
        stacked = jnp.concatenate([total[:, cols(k)] for k in range(4)], axis=0)
        zs[p, g] = dot(perm[3], stacked).astype(BF16).reshape(16, 16, W)
        for h, o, v, dz in plane:
            if h == g:
                to = (z + dz) % 8
                send(zs.at[p, g, o * 4 + v], zr.at[p, z * 4 + x], bs_sem.at[p, g, 2], br_sem.at[p, 0, 2], at(x=v, z=to))
        if g == HOME[0]:
            zr[p, z * 4 + x] = zs[p, g, HOME[1] * 4 + x]

    def g4(p):
        wait(zr.at[p, pl.ds(0, 31)], br_sem.at[p, 0, 2])
        for h in range(2):
            moved = dot(perm[2], zr[p, h * 16:(h + 1) * 16].reshape(M, W)).astype(BF16)
            for k in range(4):
                so[p, h * 64:(h + 1) * 64, cols(k)] = moved[k * 64:(k + 1) * 64]

    def w_out_grad(k):
        for s in range(2):
            gwo[s, :, cols(k)] = dot_tl(hid[s], xf[1, s, :, cols(k)]).astype(BF16)

    def w_in_grad(k):
        for s in range(2):
            gwi[s, cols(k), :] = dot_tl(xf[0, s, :, cols(k)], gpre[s]).astype(BF16)

    def combine_probs():
        e_c = jnp.exp(logits - jnp.max(logits, axis=1, keepdims=True))
        p_c = e_c / jnp.sum(e_c, axis=1, keepdims=True)
        prob_c[...] = p_c
        comb[...] = p_c.astype(BF16)
        disp_t[1] = comb[...].T

    def images_side():
        pick = one_hot(M, M, lambda i: ((i // 16) % 8) * 32 + ((i // 4) % 4) * 8 + (i // 128) * 4 + i % 4)
        for cc in range(2):
            for hh in range(2):
                pt[cc * 512 + hh * 256:cc * 512 + (hh + 1) * 256] = dot_t(
                    pick, patches[:, hh * 512 + cc * 256:hh * 512 + (cc + 1) * 256]
                ).astype(BF16)

    f0(0)
    pl.semaphore_wait(barrier, len(everyone))
    f1(0)
    for load in loads[3:]:
        load.start()
    combine_probs()
    loads[2].wait()
    f0(1)
    images_side()
    f3(0, 0)
    f1(1)
    f3(0, 1)
    f4(0, 0)
    f3(1, 0)
    loads[3].wait()
    f5(0, 0)
    gelu(0)
    loads[4].wait()
    g1(0, 0)
    f4(0, 1)
    f3(1, 1)
    g2(0, 0)
    f5(0, 1)
    gelu(1)
    g1(0, 1)
    f4(1, 0)
    g2(0, 1)
    f5(1, 0)
    grad_pre(0)
    f4(1, 1)
    g1(1, 0)
    f5(1, 1)
    grad_pre(1)
    g2(1, 0)
    g1(1, 1)
    g3(0, 0)
    g2(1, 1)
    g3(0, 1)
    w_out_grad(0)
    w_out_grad(1)
    w_out_grad(2)
    w_out_grad(3)
    g3(1, 0)
    w_in_grad(0)
    w_in_grad(1)
    g3(1, 1)
    w_in_grad(2)
    w_in_grad(3)
    g4(0)
    mixed[...] = dot(comb[...], so[0]).astype(BF16)
    p_c = prob_c[...]
    g_c = dot_t(cot[...], so[0])
    grad_c[...] = p_c * (g_c - jnp.sum(p_c * g_c, axis=1, keepdims=True))
    g4(1)
    p_d = prob_d[...]
    g_d = dot_t(patches[...], so[1])
    g_m = (grad_c[...] + p_d * (g_d - jnp.sum(p_d * g_d, axis=0, keepdims=True))).astype(BF16)

    rcs[...] = dot(pt[rows((1 - c) * 512, 512), :], g_m).astype(BF16)
    send(rcs, rcr, rs_sem.at[0], rr_sem.at[0], at(c=1 - c))
    rt[...] = dot(pt[rows(c * 512, 512), :], g_m)
    wait(rcr, rr_sem.at[0])
    rys[...] = (rt[...] + rcr[...].astype(F32)).astype(BF16).reshape(4, 128, 128)
    for v in y_ids:
        send(rys.at[v], ryr.at[y], rs_sem.at[1], rr_sem.at[1], at(y=v))
    ryr[y] = rys[y]
    wait(ryr.at[pl.ds(0, 3)], rr_sem.at[1])
    total = jnp.sum(ryr[...].astype(F32), axis=0)
    for b in range(32):
        rzs[b] = total[b * 4:(b + 1) * 4]
    for g, o, v, dz in plane:
        to = (z + dz) % 8
        send(rzs.at[to * 4 + v], rzr.at[z * 4 + x], rs_sem.at[2], rr_sem.at[2], at(x=v, z=to))
    rzr[z * 4 + x] = rzs[z * 4 + x]
    for k in range(4):
        gp[:, cols(k)] = (dot(disp[...], so[1, :, cols(k)]) + dot_t(g_m, router[cols(k), :])).astype(BF16)
    wait(rzr.at[pl.ds(0, 31)], rr_sem.at[2])
    gr_ref[...] = jnp.sum(rzr[...], axis=0).astype(BF16)

    for p in range(2):
        for g in range(2):
            wait(xr.at[p, g, pl.ds(0, 16 - (g == HOME[0]))], fs_sem.at[p, g, 0])
            wait(xf.at[p, :, pl.ds(0, 48)], fs_sem.at[p, g, 1])
            wait(xf.at[p, :, pl.ds(0, 64)], fs_sem.at[p, g, 2])
            wait(cr.at[p, g], bs_sem.at[p, g, 0])
            wait(yr.at[p, g, pl.ds(0, 3)], bs_sem.at[p, g, 1])
            wait(zs.at[p, g, pl.ds(0, 16 - (g == HOME[0]))], bs_sem.at[p, g, 2])
    wait(rcr, rs_sem.at[0])
    wait(ryr.at[pl.ds(0, 3)], rs_sem.at[1])
    wait(rzr.at[pl.ds(0, 31)], rs_sem.at[2])


def store(*refs):
    sem = refs[-1]
    copies = []
    for src, dst in zip(refs[:5], refs[5:10]):
        if src.shape[0] == 2:
            parts = [(src.at[s, pl.ds(h, src.shape[1] // 2)], dst.at[s, pl.ds(h, src.shape[1] // 2)])
                     for s in range(2) for h in (0, src.shape[1] // 2)]
        else:
            parts = [(src, dst)]
        for a, b in parts:
            copies.append(pltpu.make_async_copy(a, b, sem.at[len(copies)]))
            copies[-1].start()
    for copy in copies:
        copy.wait()


def on_device(patches, router, w_in, w_out, cotangent):
    v = pltpu.VMEM
    any_spec = pl.BlockSpec(memory_space=pl.ANY)
    shapes = ((M, D), (M, D), (4, E), (2, D, FF), (2, FF, D))
    args = [
        pltpu.with_memory_space_constraint(a, pltpu.HBM)
        for a in (patches[0], router, w_in, w_out, cotangent[0])
    ]
    results = pl.pallas_call(
        kernel,
        name="soft_moe",
        out_shape=tuple(v(s, BF16) for s in shapes),
        in_specs=[any_spec] * 5,
        out_specs=[pl.BlockSpec(memory_space=pltpu.VMEM)] * 5,
        scratch_shapes=[
            v((M, D), BF16), v((D, E), BF16), v((2, D, FF), BF16), v((2, FF, D), BF16), v((M, D), BF16),
            v((4, M, M), BF16), v((D, M), BF16), v((M, E), F32), v((M, E), F32),
            v((2, E, M), BF16), v((M, E), BF16), v((M, E), BF16),
            v((2, 2, M, W), BF16), v((2, 32, 16, W), BF16), v((2, 2, 16, 16, W), BF16), v((2, 2, 4, 16, D), BF16),
            v((2, 2, 256, D), BF16),
            v((2, 2, 256, FF), F32), v((2, 256, FF), F32), v((2, 256, FF), BF16), v((2, 256, FF), BF16),
            v((2, 2, 2, 128, D), F32), v((2, 2, 2, 64, D), BF16), v((2, 2, 2, 64, D), BF16),
            v((2, 2, 4, 2, 16, D), BF16), v((2, 2, 4, 2, 16, D), BF16),
            v((2, 2, 16, 16, W), BF16), v((2, 32, 16, W), BF16), v((2, E, D), BF16),
            v((M, E), F32),
            v((512, E), F32), v((512, E), BF16), v((512, E), BF16), v((4, 128, E), BF16), v((4, 128, E), BF16),
            v((32, 4, E), F32), v((32, 4, E), F32),
            pltpu.SemaphoreType.DMA((5,)),
            pltpu.SemaphoreType.DMA((2, 2, 3)), pltpu.SemaphoreType.DMA((2, 2, 3)),
            pltpu.SemaphoreType.DMA((2, 2, 3)), pltpu.SemaphoreType.DMA((2, 2, 3)),
            pltpu.SemaphoreType.DMA((3,)), pltpu.SemaphoreType.DMA((3,)),
        ],
        compiler_params=pltpu.CompilerParams(
            collective_id=0, has_side_effects=True, vmem_limit_bytes=44 * 2**20
        ),
        cost_estimate=pl.CostEstimate(flops=4_700_000_000, bytes_accessed=13_000_000, transcendentals=500_000),
    )(*args)
    mixed, gp, gr, gwi, gwo = pl.pallas_call(
        store,
        name="store",
        out_shape=tuple(jax.ShapeDtypeStruct(s, BF16) for s in shapes),
        in_specs=[pl.BlockSpec(memory_space=pltpu.VMEM)] * 5,
        out_specs=[any_spec] * 5,
        scratch_shapes=[pltpu.SemaphoreType.DMA((11,))],
        compiler_params=pltpu.CompilerParams(vmem_limit_bytes=4 * 2**20),
    )(*[pltpu.with_memory_space_constraint(a, pltpu.VMEM) for a in results])
    return mixed[None], gp[None], gr, gwi, gwo


def solution(mesh):
    placed = (
        P(("dp", "expert"), None, None),
        P(),
        P("expert", None, "dp"),
        P("expert", "dp", None),
        P(("dp", "expert"), None, None),
    )
    return jax.shard_map(
        on_device,
        mesh=mesh,
        in_specs=placed,
        out_specs=(
            P(("dp", "expert"), None, None),
            P(("dp", "expert"), None, None),
            P(("dp", "expert"), None),
            P("expert", None, "dp"),
            P("expert", "dp", None),
        ),
        check_vma=False,
    )
```
